128 devices in a mesh: lat: 16 (over x, y_lo, core), dep: 8 (over y_hi, z).
Axes of the slice: x: 4, y: 4 (y_hi: 2, y_lo: 2; y = y_hi * 2 + y_lo), z: 4, core: 2. Of those that a mesh axis runs over, the one named last changes fastest.
Arguments:
- crystal: float32 [2, 128, 4096, 256], P(None, 'dep', 'lat'), may hold values from -6 to 6
- beam_probe: float32 [2, 256, 256], replicated, may hold values from -1.25 to 1.25
- amplitudes: float32 [128, 256, 256], P('lat'), may hold values from 0.2 to 3
- starts: int32 [128], P('lat'), may hold values from 0 to 127
- shears: int32 [128], P('dep'), may hold values from -32 to 32
Outputs:
- updated: float32 [2, 128, 4096, 256], P(None, 'dep', 'lat')
The draws below stay inside these ranges and needn't reach their ends.
All inputs are finite; a program needn't handle non-finite values.
Results may differ from the reference program's by a relative error of at most 0.0003.
Values sent between devices are 32-bit elements; how exact they have to be, the bound alone decides.
No kernel may reach another device: no remote copies, remote signals or barrier semaphores. Data moves between devices by JAX's collectives and lax.ppermute only.
A program may use at most 192 MiB of HBM per device.

```python
import math
import jax
import jax.numpy as jnp
from jax import lax

W = 256
BX = 256
SH = 32
POS_DEV = 8
RR = 160
NZ = 128
NX = 4096
POSITIONS = 128


def draw_starts(key, part):
    key = jax.random.fold_in(key, 11)
    first, second = jax.random.split(key)
    values = jax.random.randint(first, (POSITIONS,), 0, BX // 2, dtype=jnp.int32)
    order = jax.random.permutation(second, POSITIONS)
    values = values.at[order[0]].set(BX // 2 - 1)
    values = values.at[order[1]].set(0)
    return values.astype(jnp.int32)


def draw_shears(key, part):
    key = jax.random.fold_in(key, 23)
    first, second = jax.random.split(key)
    values = jax.random.randint(first, (NZ,), 0 - SH, SH + 1, dtype=jnp.int32)
    order = jax.random.permutation(second, NZ)
    values = values.at[order[0]].set(SH)
    values = values.at[order[1]].set(0 - SH)
    return values.astype(jnp.int32)


def block_scale(key, extent, cuts, low, largest):
    def one(position, shards_of):
        draws = jax.random.uniform(jax.random.fold_in(jax.random.fold_in(key, 6), position), (shards_of,), jnp.float32, low / len(cuts), largest / len(cuts))
        return jnp.repeat(jnp.exp(draws), extent[position] // shards_of).reshape((-1,) + (1,) * (len(extent) - position - 1))

    level = one(*cuts[0])
    for cut in cuts[1:]:
        level = level * one(*cut)
    return level


def gaussian(own_key, dims, width, most, pieces=(), kind=jnp.bfloat16):
    array = jax.random.normal(own_key, dims, jnp.float32) * width
    if len(pieces) > 0:
        array = block_scale(own_key, dims, pieces, -0.22, 0.18) * array
    return jnp.clip(array, min=-most, max=most).astype(kind)


def setup_inputs(seed: int = 0) -> dict:
    seeds = jax.random.split(jax.random.key(seed), 6)
    crystal = gaussian(seeds[0], (2, NZ, NX, W), 1.0, 6.0, ((1, 8), (2, 16)), jnp.float32)
    beam_probe = gaussian(seeds[1], (2, W, W), (1.0 / NZ ** 0.5), 1.25, (), jnp.float32)
    amplitudes = jnp.clip(jnp.exp(math.log(3.0) - 2.7080502 * jax.random.uniform(seeds[2], (POSITIONS, W, W), jnp.float32) ** block_scale(seeds[2], (POSITIONS, W, W), ((0, 16),), -0.2, 0.2)), 0.2, 3.0)
    starts = draw_starts(jax.random.fold_in(seeds[5], 71), 0)
    shears = draw_shears(jax.random.fold_in(seeds[5], 71), 0)
    return {"crystal": crystal, "beam_probe": beam_probe, "amplitudes": amplitudes, "starts": starts, "shears": shears}


step_size = 0.5
amp_floor = 0.5


def reference(crystal, beam_probe, amplitudes, starts, shears):
    padded = jnp.pad(crystal, ((0, 0), (0, 0), (SH, RR), (0, 0)))
    owners = jnp.arange(POSITIONS, dtype=jnp.int32) // POS_DEV
    anchors = (owners * BX + starts + SH).astype(jnp.int32)
    zero = jnp.zeros((), jnp.int32)
    probe_re = beam_probe[0]
    probe_im = beam_probe[1]
    peak = jnp.max(probe_re * probe_re + probe_im * probe_im)

    def column(anchor):
        def add_layer(z, total):
            z = jnp.asarray(z).astype(jnp.int32)
            offset = (anchor + shears[z]).astype(jnp.int32)
            piece = lax.dynamic_slice(padded, (zero, z, offset, zero), (2, 1, W, W))
            return total + piece[:, 0]
        return lax.fori_loop(0, NZ, add_layer, jnp.zeros((2, W, W), jnp.float32))

    def difference(anchor, amp):
        col = column(anchor)
        wave_re = probe_re * col[0] - probe_im * col[1]
        wave_im = probe_re * col[1] + probe_im * col[0]
        wave = wave_re + 1j * wave_im
        far_field = jnp.fft.fft2(wave, norm="ortho")
        modulus = jnp.abs(far_field)
        projected = amp * far_field / jnp.maximum(modulus, amp_floor)
        back = jnp.fft.ifft2(projected, norm="ortho") - wave
        diff_re = jnp.real(back).astype(wave_re.dtype)
        diff_im = jnp.imag(back).astype(wave_re.dtype)
        change_re = step_size * (probe_re * diff_re + probe_im * diff_im) / peak
        change_im = step_size * (probe_re * diff_im - probe_im * diff_re) / peak
        return jnp.stack([change_re, change_im])

    def per_position(totals, inputs):
        anchor, amp = inputs
        change = difference(anchor, amp)

        def put_layer(z, acc):
            z = jnp.asarray(z).astype(jnp.int32)
            offset = (anchor + shears[z]).astype(jnp.int32)
            current = lax.dynamic_slice(acc, (zero, z, offset, zero), (2, 1, W, W))
            return lax.dynamic_update_slice(acc, current + change[:, None], (zero, z, offset, zero))
        return lax.fori_loop(0, NZ, put_layer, totals), None

    totals, unused = lax.scan(per_position, jnp.zeros_like(padded), (anchors, amplitudes))
    return crystal + totals[:, :, SH:SH + NX, :]
```

```python
import functools
import math

import jax
import jax.numpy as jnp
import ml_dtypes
import numpy as np
from jax import lax
from jax.experimental import pallas as pl
from jax.experimental.pallas import tpu as pltpu
from jax.sharding import PartitionSpec as P

BX = 256
SH = 32
HALF = 128
QUARTER = 64
WIDE = 320
PART = 160
FULL = 384
DEP = 8

step_size = 0.5
amp_floor = 0.5
f32 = jnp.float32
bf16 = jnp.bfloat16
VMEM_LIMIT = 24 * 1024 * 1024


def vmem():
    return pl.BlockSpec(memory_space=pltpu.VMEM)


def smem():
    return pl.BlockSpec(memory_space=pltpu.SMEM)


def anywhere():
    return pl.BlockSpec(memory_space=pl.ANY)


def params():
    return pltpu.CompilerParams(vmem_limit_bytes=VMEM_LIMIT)


def kept(shape):
    return pltpu.VMEM(shape, f32)


def held(*arrays):
    return tuple(pltpu.with_memory_space_constraint(a, pltpu.VMEM) for a in arrays)


def split_np(table):
    high = table.astype(ml_dtypes.bfloat16).astype(np.float64)
    low = table - high
    return high, low


def tables(sets):
    size = BX // sets
    u = np.arange(size)
    forward, inverse = [], []
    for q in range(sets):
        angle = 2.0 * math.pi * ((u[None, :] * (sets * u[:, None] + q)) % BX) / BX
        cos, sin = np.cos(angle) / 16.0, np.sin(angle) / 16.0
        forward.append(np.block([[cos, sin], [-sin, cos]]))
        inverse.append(np.block([[cos.T, -sin.T], [sin.T, cos.T]]))
    return forward + inverse


def packed_tables():
    def beside(m, axis):
        h, l = split_np(m)
        return np.concatenate([h, h, l], axis=axis)

    lefts = np.stack([beside(m, 1) for m in tables(4)])
    rights = np.stack([beside(m.T, 0) for m in tables(2)])
    order = np.concatenate([np.arange(0, BX, 2), np.arange(1, BX, 2)])
    pick = np.zeros((BX, BX))
    pick[order, np.arange(BX)] = 1.0
    return tuple(jnp.asarray(m.astype(ml_dtypes.bfloat16)) for m in (lefts, rights, pick))


def place():
    z = lax.axis_index("dep") % 4
    return z // 2, z % 2


def partial_kernel(other, shears_in, crystal, *rest):
    first, second, buf, shears, sems, shears_sem = rest[-6:]
    shears_copy = pltpu.make_async_copy(shears_in, shears, shears_sem)
    shears_copy.start()
    half, part = place()
    half = 1 - half if other else half
    part = part if other else 1 - part
    layers = buf.shape[1]
    group = 4
    lanes = pl.ds(pl.multiple_of(half * HALF, HALF), HALF)
    copies = []
    for g in range(layers // group):
        copy = pltpu.make_async_copy(
            crystal.at[:, pl.ds(g * group, group), :, lanes],
            buf.at[:, pl.ds(g * group, group), pl.ds(2 * SH, BX), :],
            sems.at[g],
        )
        copy.start()
        copies.append(copy)
    pad = jnp.zeros((2, layers, 2 * SH, HALF), f32)
    buf[:, :, : 2 * SH, :] = pad
    buf[:, :, 2 * SH + BX :, :] = pad
    shears_copy.wait()
    for g in range(layers // group):
        copies[g].wait()
        for out, c in ((first, part), (second, 1 - part)):
            total = None if g == 0 else out[...]
            for i in range(group):
                z = g * group + i
                piece = buf[c, z, pl.ds(SH + shears[z], WIDE), :]
                total = piece if total is None else total + piece
            out[...] = total


def partial_sums(crystal, shears, other, *after):
    layers = crystal.shape[1]
    block = kept((WIDE, HALF))
    return pl.pallas_call(
        functools.partial(partial_kernel, other),
        out_shape=(block, block, kept((2, layers, BX + 4 * SH, HALF))),
        in_specs=[anywhere()] * (2 + len(after)),
        out_specs=(vmem(), vmem(), vmem()),
        scratch_shapes=[
            pltpu.SMEM(shears.shape, jnp.int32),
            pltpu.SemaphoreType.DMA((layers // 4,)),
            pltpu.SemaphoreType.DMA,
        ],
        compiler_params=params(),
    )(*(pltpu.with_memory_space_constraint(a, pltpu.HBM) for a in (shears, crystal)), *held(*after))


def sum_kernel(a, b, c, d, unused, out):
    out[...] = (a[...] + b[...]) + (c[...] + d[...])


def sum_blocks(*blocks):
    return pl.pallas_call(
        sum_kernel,
        out_shape=kept(blocks[0].shape),
        in_specs=[vmem()] * 4 + [anywhere()],
        out_specs=vmem(),
        compiler_params=params(),
    )(*held(*blocks))


def edges_kernel(own, own2, out, to_left, to_right):
    total = own[...] + own2[...]
    out[...] = total
    to_left[...] = total[:PART]
    to_right[...] = total[WIDE - SH :]


def edges(*blocks):
    return pl.pallas_call(
        edges_kernel,
        out_shape=(kept((WIDE, HALF)), kept((PART, HALF)), kept((SH, HALF))),
        in_specs=[vmem()] * 2,
        out_specs=(vmem(), vmem(), vmem()),
        compiler_params=params(),
    )(*held(*blocks))


def finish_kernel(own, left, right, out):
    out[: WIDE - SH, :] = own[SH:, :]
    out[WIDE - SH :, :] = jnp.zeros((FULL - WIDE + SH, HALF), f32)
    out[:SH, :] += left[...]
    out[FULL - PART :, :] += right[...]


def finish(*blocks):
    return pl.pallas_call(
        finish_kernel,
        out_shape=kept((FULL, HALF)),
        in_specs=[vmem()] * 3,
        out_specs=vmem(),
        compiler_params=params(),
    )(*held(*blocks))


def split3(x):
    a = x.astype(bf16)
    r = x - a.astype(f32)
    b = r.astype(bf16)
    return a, b, (r - b.astype(f32)).astype(bf16)


def prepare_kernel(amps, probe, pick, amps_out, back_out, moved):
    table = pick[...]

    def one(p, carry):
        a, b, c = split3(amps[p])
        total = (
            jnp.dot(a, table, preferred_element_type=f32)
            + jnp.dot(b, table, preferred_element_type=f32)
            + jnp.dot(c, table, preferred_element_type=f32)
        )
        for h in range(2):
            lanes = slice(h * HALF, (h + 1) * HALF)
            moved[h] = total[:, lanes]
            for q in range(4):
                amps_out[p, q * QUARTER : (q + 1) * QUARTER, lanes] = moved[h, pl.ds(q, QUARTER, stride=4), :]
        return carry

    lax.fori_loop(0, amps.shape[0], one, 0)
    re, im = probe[0], probe[1]
    peak = jnp.max(re * re + im * im)
    back_out[0] = step_size * re / peak
    back_out[1] = step_size * im / peak


def prepare(amplitudes, beam_probe, pick):
    return pl.pallas_call(
        prepare_kernel,
        out_shape=(kept(amplitudes.shape), kept(beam_probe.shape)),
        in_specs=[vmem()] * 3,
        out_specs=(vmem(), vmem()),
        scratch_shapes=[pltpu.VMEM((2, BX, HALF), f32)],
        compiler_params=params(),
    )(*held(amplitudes, beam_probe, pick))


def split2(x):
    a = x.astype(bf16)
    return a, (x - a.astype(f32)).astype(bf16)


def along_rows(table, stacked):
    high, low = split2(stacked)
    return jnp.dot(table, jnp.concatenate([high, low, high], axis=0), preferred_element_type=f32)


def along_lanes(stacked, table):
    high, low = split2(stacked)
    return jnp.dot(jnp.concatenate([high, low, high], axis=1), table, preferred_element_type=f32)


def lanes_of(turn):
    half, _ = place()
    return pl.ds(pl.multiple_of((half ^ turn) * HALF, HALF), HALF)


def fill(t, own, other):
    _, part = place()
    t[part] = own[...]
    t[1 - part] = other[...]


def both(first, second):
    return [a + b for a, b in zip(first, second)], [a - b for a, b in zip(first, second)]


def stack_rows(*parts):
    return jnp.concatenate(parts, axis=0)


def row_bins(turn, pair, starts, t, probe, lefts):
    lanes = lanes_of(turn)
    sets = [[], [], [], []]
    for p in pair:
        s = starts[p]
        re, im = t[0, pl.ds(s, BX), :], t[1, pl.ds(s, BX), :]
        pr, pi = probe[0, :, lanes], probe[1, :, lanes]
        waves = (pr * re - pi * im, pr * im + pi * re)
        s0, s1 = both([w[:QUARTER] for w in waves], [w[HALF : HALF + QUARTER] for w in waves])
        t0, t1 = both([w[QUARTER:HALF] for w in waves], [w[HALF + QUARTER :] for w in waves])
        sets[0].append(stack_rows(s0[0] + t0[0], s0[1] + t0[1]))
        sets[1].append(stack_rows(s1[0] + t1[1], s1[1] - t1[0]))
        sets[2].append(stack_rows(s0[0] - t0[0], s0[1] - t0[1]))
        sets[3].append(stack_rows(s1[0] - t1[1], s1[1] + t1[0]))
    bins = [along_rows(lefts[q], jnp.concatenate(sets[q], axis=1)) for q in range(4)]
    return [[b[:, j * HALF : (j + 1) * HALF] for b in bins] for j in range(2)]


def first_kernel(starts, own, one, probe, lefts, out, t):
    fill(t, own, one)

    def pair(i, carry):
        for j, bins in enumerate(row_bins(0, (2 * i, 2 * i + 1), starts, t, probe, lefts)):
            for q in range(4):
                out[2 * i + j, q] = bins[q]
        return carry

    lax.fori_loop(0, starts.shape[0] // 2, pair, 0, unroll=2)


def first_half(starts, own, one, beam_probe, lefts):
    return pl.pallas_call(
        first_kernel,
        out_shape=kept((starts.shape[0], 4, 2 * QUARTER, HALF)),
        in_specs=[smem()] + [vmem()] * 4,
        out_specs=vmem(),
        scratch_shapes=[pltpu.VMEM((2, FULL, HALF), f32)],
        compiler_params=params(),
    )(starts, *held(own, one, beam_probe, lefts))


def positions_kernel(starts, mine, two, three, probe, back, amps, lefts, rights, g_out, right_out, left_out, t):
    fill(t, two, three)
    g_out[...] = jnp.zeros(g_out.shape, f32)
    sides = (slice(0, HALF), slice(HALF, BX))
    count = starts.shape[0]
    bins, far_field, change = {}, {}, {}

    def lanes_forward(p):
        even, odd = [], []
        for a, b in zip([mine[p, q] for q in range(4)], bins.pop(p)):
            total, rest = a + b, a - b
            even.append(jnp.concatenate([total[:QUARTER], total[QUARTER:]], axis=1))
            odd.append(jnp.concatenate([rest[:QUARTER], rest[QUARTER:]], axis=1))
        far_field[p] = [along_lanes(stack_rows(*rows), rights[lp]) for lp, rows in ((0, even), (1, odd))]

    def project(p):
        backs = []
        for lp, f in enumerate(far_field.pop(p)):
            fr, fi = f[:, :HALF], f[:, HALF:]
            modulus2 = jnp.maximum(fr * fr + fi * fi, amp_floor * amp_floor)
            factor = amps[p, :, sides[lp]] * lax.rsqrt(modulus2) - 1.0
            backs.append(along_lanes(jnp.concatenate([fr * factor, fi * factor], axis=1), rights[2 + lp]))
        change[p] = backs[0] + backs[1], backs[0] - backs[1]

    def rows_back(p):
        s = starts[p]
        low, high = change.pop(p)
        sets = []
        for q in range(4):
            at = slice(q * QUARTER, (q + 1) * QUARTER)
            stacked = [jnp.concatenate([low[at, side], high[at, side]], axis=1) for side in sides]
            g = along_rows(lefts[4 + q], stack_rows(*stacked))
            sets.append((g[:QUARTER], g[QUARTER:]))
        s0, s1 = both(sets[0], sets[2])
        t0, t1 = both(sets[1], sets[3])
        diff_re = stack_rows(s0[0] + t0[0], s1[0] - t1[1], s0[0] - t0[0], s1[0] + t1[1])
        diff_im = stack_rows(s0[1] + t0[1], s1[1] + t1[0], s0[1] - t0[1], s1[1] - t1[0])
        for turn in range(2):
            dr, di = diff_re[:, sides[turn]], diff_im[:, sides[turn]]
            br, bi = back[0, :, lanes_of(turn)], back[1, :, lanes_of(turn)]
            g_out[0, turn, pl.ds(s, BX), :] += br * dr + bi * di
            g_out[1, turn, pl.ds(s, BX), :] += br * di - bi * dr

    for step in range(count + 3):
        if step < count and step % 2 == 0:
            pair = (step, step + 1)
            bins.update(zip(pair, row_bins(1, pair, starts, t, probe, lefts)))
        if 0 <= step - 1 < count:
            lanes_forward(step - 1)
        if 0 <= step - 2 < count:
            project(step - 2)
        if 0 <= step - 3:
            rows_back(step - 3)
    right_out[...] = g_out[:, :, BX - SH :, :]
    left_out[...] = g_out[:, :, :SH, :]


def positions(starts, mine, two, three, beam_probe, back, amps, lefts, rights):
    return pl.pallas_call(
        positions_kernel,
        out_shape=(kept((2, 2, FULL, HALF)), kept((2, 2, PART, HALF)), kept((2, 2, SH, HALF))),
        in_specs=[smem()] + [vmem()] * 8,
        out_specs=(vmem(), vmem(), vmem()),
        scratch_shapes=[pltpu.VMEM((2, FULL, HALF), f32)],
        compiler_params=params(),
    )(starts, *held(mine, two, three, beam_probe, back, amps, lefts, rights))


EARLY = 3
CHUNKS = BX // SH


def first_early(shear):
    return 3 + (shear > -SH).astype(jnp.int32) + (shear > 0).astype(jnp.int32)


def rows_at(chunk, count, before=0):
    return pl.ds(pl.multiple_of(chunk * SH, SH) + before, count * SH)


def update_layer(z, chunk, count, shear, far, own, changes, before, buf, at):
    for c in range(2):
        for turn, source in enumerate((own, far)):
            cells = source[c, z, rows_at(chunk, count, 2 * SH), :]
            moved = changes[c, turn, pl.ds(chunk * SH + before - shear, count * SH), :]
            buf[c, z, at * SH : (at + count) * SH, lanes_of(turn)] = cells + moved


def send_rows(z, chunk, count, buf, at, out, sem):
    source = buf.at[:, z, pl.ds(at * SH, count * SH), :]
    pltpu.make_async_copy(source, out.at[:, z, rows_at(chunk, count), :], sem).start()


def early_kernel(shears, far, own, g, out, buf, sem):
    def layer(z, carry):
        chunk = first_early(shears[z])
        update_layer(z, chunk, EARLY, shears[z], far, own, g, 0, buf, 0)
        send_rows(z, chunk, EARLY, buf, 0, out, sem)
        return carry

    lax.fori_loop(0, buf.shape[1], layer, 0)
    pltpu.make_async_copy(buf, out.at[:, :, : EARLY * SH, :], sem).wait()


def update_kernel(shears, far, own, g, left, right, begun, out, ext, buf, sem):
    ext[:, :, SH:, :] = g[:, :, : BX + SH, :]
    ext[:, :, :SH, :] = jnp.zeros((2, 2, SH, HALF), f32)
    ext[:, :, :PART, :] += left[...]
    ext[:, :, BX + SH :, :] += right[...]

    def layer(z, carry):
        begin = first_early(shears[z])
        pieces = (
            (0, 3),
            (jnp.where(begin == 3, 6, 3), 1),
            (jnp.where(begin == 5, 4, 7), 1),
        )
        at = 0
        for chunk, count in pieces:
            update_layer(z, chunk, count, shears[z], far, own, ext, SH, buf, at)
            send_rows(z, chunk, count, buf, at, out, sem)
            at += count
        return carry

    lax.fori_loop(0, buf.shape[1], layer, 0)
    pltpu.make_async_copy(buf, out.at[:, :, : (CHUNKS - EARLY) * SH, :], sem).wait()


def update_early(far, own, shears, g):
    layers = far.shape[1]
    return pl.pallas_call(
        early_kernel,
        out_shape=pltpu.HBM((2, layers, BX, BX), f32),
        in_specs=[smem()] + [vmem()] * 3,
        out_specs=pl.BlockSpec(memory_space=pltpu.HBM),
        scratch_shapes=[pltpu.VMEM((2, layers, EARLY * SH, BX), f32), pltpu.SemaphoreType.DMA],
        compiler_params=params(),
    )(shears, *held(far, own, g))


def update(far, own, shears, g, left, right, begun):
    layers = far.shape[1]
    return pl.pallas_call(
        update_kernel,
        out_shape=jax.ShapeDtypeStruct((2, layers, BX, BX), f32),
        in_specs=[smem()] + [vmem()] * 5 + [pl.BlockSpec(memory_space=pltpu.HBM)],
        out_specs=pl.BlockSpec(memory_space=pltpu.HBM),
        input_output_aliases={6: 0},
        scratch_shapes=[
            pltpu.VMEM((2, 2, BX + 2 * SH, HALF), f32),
            pltpu.VMEM((2, layers, (CHUNKS - EARLY) * SH, BX), f32),
            pltpu.SemaphoreType.DMA,
        ],
        compiler_params=params(),
    )(shears, *held(far, own, g, left, right), begun)


def depth_swap(value, by):
    return lax.ppermute(value, "dep", [(i, i ^ by) for i in range(DEP)])


def shifted(value, by):
    count = lax.axis_size("lat")
    return lax.ppermute(value, "lat", [(i, i + by) for i in range(count) if 0 <= i + by < count])


def body(crystal, beam_probe, amplitudes, starts, shears):
    lefts, rights, pick = packed_tables()
    send2, send3, far = partial_sums(crystal, shears, True)
    got3 = depth_swap(send3, 3)
    got2 = depth_swap(send2, 2)
    send1, mine, near_half = partial_sums(crystal, shears, False, send2)
    got1 = depth_swap(send1, 1)
    amps, back = prepare(amplitudes, beam_probe, pick)
    part = sum_blocks(mine, got1, got2, got3, back)
    whole, to_left, to_right = edges(part, depth_swap(part, 4))
    block = finish(whole, shifted(to_right, 1), shifted(to_left, -1))
    three = depth_swap(block, 3)
    two = depth_swap(block, 2)
    one = depth_swap(block, 1)
    bins = first_half(starts, block, one, beam_probe, lefts)
    g, to_right, to_left = positions(starts, bins, two, three, beam_probe, back, amps, lefts, rights)
    begun = update_early(far, near_half, shears, g)
    return update(far, near_half, shears, g, shifted(to_right, 1), shifted(to_left, -1), begun)


def solution(mesh):
    placed = (P(None, "dep", "lat", None), P(), P("lat", None, None), P("lat"), P("dep"))
    return jax.shard_map(
        body, mesh=mesh, in_specs=placed, out_specs=P(None, "dep", "lat", None), check_vma=False
    )
```

```python
import functools
import math

import jax
import jax.numpy as jnp
import ml_dtypes
import numpy as np
from jax import lax
from jax.experimental import pallas as pl
from jax.experimental.pallas import tpu as pltpu
from jax.sharding import PartitionSpec as P

BX = 256
SH = 32
HALF = 128
QUARTER = 64
WIDE = 320
PART = 160
FULL = 384
DEP = 8

step_size = 0.5
amp_floor = 0.5
f32 = jnp.float32
bf16 = jnp.bfloat16
VMEM_LIMIT = 24 * 1024 * 1024


def vmem():
    return pl.BlockSpec(memory_space=pltpu.VMEM)


def smem():
    return pl.BlockSpec(memory_space=pltpu.SMEM)


def anywhere():
    return pl.BlockSpec(memory_space=pl.ANY)


def params():
    return pltpu.CompilerParams(vmem_limit_bytes=VMEM_LIMIT)


def kept(shape):
    return pltpu.VMEM(shape, f32)


def held(*arrays):
    return tuple(pltpu.with_memory_space_constraint(a, pltpu.VMEM) for a in arrays)


def split_np(table):
    high = table.astype(ml_dtypes.bfloat16).astype(np.float64)
    low = table - high
    return high, low


def tables(sets):
    size = BX // sets
    u = np.arange(size)
    forward, inverse = [], []
    for q in range(sets):
        angle = 2.0 * math.pi * ((u[None, :] * (sets * u[:, None] + q)) % BX) / BX
        cos, sin = np.cos(angle) / 16.0, np.sin(angle) / 16.0
        forward.append(np.block([[cos, sin], [-sin, cos]]))
        inverse.append(np.block([[cos.T, -sin.T], [sin.T, cos.T]]))
    return forward + inverse


def packed_tables():
    def beside(m, axis):
        h, l = split_np(m)
        return np.concatenate([h, h, l], axis=axis)

    lefts = np.stack([beside(m, 1) for m in tables(4)])
    rights = np.stack([beside(m.T, 0) for m in tables(2)])
    order = np.concatenate([np.arange(0, BX, 2), np.arange(1, BX, 2)])
    pick = np.zeros((BX, BX))
    pick[order, np.arange(BX)] = 1.0
    return tuple(jnp.asarray(m.astype(ml_dtypes.bfloat16)) for m in (lefts, rights, pick))


def place():
    z = lax.axis_index("dep") % 4
    return z // 2, z % 2


def partial_kernel(other, shears_in, crystal, *rest):
    first, second, buf, shears, sems, shears_sem = rest[-6:]
    shears_copy = pltpu.make_async_copy(shears_in, shears, shears_sem)
    shears_copy.start()
    half, part = place()
    half = 1 - half if other else half
    part = part if other else 1 - part
    layers = buf.shape[1]
    group = 2
    lanes = pl.ds(pl.multiple_of(half * HALF, HALF), HALF)
    copies = []
    for g in range(layers // group):
        copy = pltpu.make_async_copy(
            crystal.at[:, pl.ds(g * group, group), :, lanes],
            buf.at[:, pl.ds(g * group, group), pl.ds(2 * SH, BX), :],
            sems.at[g],
        )
        copy.start()
        copies.append(copy)
    pad = jnp.zeros((2, layers, 2 * SH, HALF), f32)
    buf[:, :, : 2 * SH, :] = pad
    buf[:, :, 2 * SH + BX :, :] = pad
    shears_copy.wait()
    for g in range(layers // group):
        copies[g].wait()
        for out, c in ((first, part), (second, 1 - part)):
            total = None if g == 0 else out[...]
            for i in range(group):
                z = g * group + i
                piece = buf[c, z, pl.ds(SH + shears[z], WIDE), :]
                total = piece if total is None else total + piece
            out[...] = total


def partial_sums(crystal, shears, other, *after):
    layers = crystal.shape[1]
    block = kept((WIDE, HALF))
    return pl.pallas_call(
        functools.partial(partial_kernel, other),
        out_shape=(block, block, kept((2, layers, BX + 4 * SH, HALF))),
        in_specs=[anywhere()] * (2 + len(after)),
        out_specs=(vmem(), vmem(), vmem()),
        scratch_shapes=[
            pltpu.SMEM(shears.shape, jnp.int32),
            pltpu.SemaphoreType.DMA((layers // 2,)),
            pltpu.SemaphoreType.DMA,
        ],
        compiler_params=params(),
    )(*(pltpu.with_memory_space_constraint(a, pltpu.HBM) for a in (shears, crystal)), *held(*after))


def sum_kernel(a, b, c, d, unused, out):
    out[...] = (a[...] + b[...]) + (c[...] + d[...])


def sum_blocks(*blocks):
    return pl.pallas_call(
        sum_kernel,
        out_shape=kept(blocks[0].shape),
        in_specs=[vmem()] * 4 + [anywhere()],
        out_specs=vmem(),
        compiler_params=params(),
    )(*held(*blocks))


def edges_kernel(own, own2, out, to_left, to_right):
    total = own[...] + own2[...]
    out[...] = total
    to_left[...] = total[:PART]
    to_right[...] = total[WIDE - SH :]


def edges(*blocks):
    return pl.pallas_call(
        edges_kernel,
        out_shape=(kept((WIDE, HALF)), kept((PART, HALF)), kept((SH, HALF))),
        in_specs=[vmem()] * 2,
        out_specs=(vmem(), vmem(), vmem()),
        compiler_params=params(),
    )(*held(*blocks))


def finish_kernel(own, left, right, out):
    out[: WIDE - SH, :] = own[SH:, :]
    out[WIDE - SH :, :] = jnp.zeros((FULL - WIDE + SH, HALF), f32)
    out[:SH, :] += left[...]
    out[FULL - PART :, :] += right[...]


def finish(*blocks):
    return pl.pallas_call(
        finish_kernel,
        out_shape=kept((FULL, HALF)),
        in_specs=[vmem()] * 3,
        out_specs=vmem(),
        compiler_params=params(),
    )(*held(*blocks))


def split3(x):
    a = x.astype(bf16)
    r = x - a.astype(f32)
    b = r.astype(bf16)
    return a, b, (r - b.astype(f32)).astype(bf16)


def prepare_kernel(amps, probe, pick, amps_out, back_out, moved):
    table = pick[...]

    def one(p, carry):
        a, b, c = split3(amps[p])
        total = (
            jnp.dot(a, table, preferred_element_type=f32)
            + jnp.dot(b, table, preferred_element_type=f32)
            + jnp.dot(c, table, preferred_element_type=f32)
        )
        for h in range(2):
            lanes = slice(h * HALF, (h + 1) * HALF)
            moved[h] = total[:, lanes]
            for q in range(4):
                amps_out[p, q * QUARTER : (q + 1) * QUARTER, lanes] = moved[h, pl.ds(q, QUARTER, stride=4), :]
        return carry

    lax.fori_loop(0, amps.shape[0], one, 0)
    re, im = probe[0], probe[1]
    peak = jnp.max(re * re + im * im)
    back_out[0] = step_size * re / peak
    back_out[1] = step_size * im / peak


def prepare(amplitudes, beam_probe, pick):
    return pl.pallas_call(
        prepare_kernel,
        out_shape=(kept(amplitudes.shape), kept(beam_probe.shape)),
        in_specs=[vmem()] * 3,
        out_specs=(vmem(), vmem()),
        scratch_shapes=[pltpu.VMEM((2, BX, HALF), f32)],
        compiler_params=params(),
    )(*held(amplitudes, beam_probe, pick))


def split2(x):
    a = x.astype(bf16)
    return a, (x - a.astype(f32)).astype(bf16)


def along_rows(table, stacked):
    high, low = split2(stacked)
    return jnp.dot(table, jnp.concatenate([high, low, high], axis=0), preferred_element_type=f32)


def along_lanes(stacked, table):
    high, low = split2(stacked)
    return jnp.dot(jnp.concatenate([high, low, high], axis=1), table, preferred_element_type=f32)


def lanes_of(turn):
    half, _ = place()
    return pl.ds(pl.multiple_of((half ^ turn) * HALF, HALF), HALF)


def fill(t, own, other):
    _, part = place()
    t[part] = own[...]
    t[1 - part] = other[...]


def both(first, second):
    return [a + b for a, b in zip(first, second)], [a - b for a, b in zip(first, second)]


def stack_rows(*parts):
    return jnp.concatenate(parts, axis=0)


def row_bins(turn, pair, starts, t, probe, lefts):
    lanes = lanes_of(turn)
    sets = [[], [], [], []]
    for p in pair:
        s = starts[p]
        re, im = t[0, pl.ds(s, BX), :], t[1, pl.ds(s, BX), :]
        pr, pi = probe[0, :, lanes], probe[1, :, lanes]
        waves = (pr * re - pi * im, pr * im + pi * re)
        s0, s1 = both([w[:QUARTER] for w in waves], [w[HALF : HALF + QUARTER] for w in waves])
        t0, t1 = both([w[QUARTER:HALF] for w in waves], [w[HALF + QUARTER :] for w in waves])
        sets[0].append(stack_rows(s0[0] + t0[0], s0[1] + t0[1]))
        sets[1].append(stack_rows(s1[0] + t1[1], s1[1] - t1[0]))
        sets[2].append(stack_rows(s0[0] - t0[0], s0[1] - t0[1]))
        sets[3].append(stack_rows(s1[0] - t1[1], s1[1] + t1[0]))
    bins = [along_rows(lefts[q], jnp.concatenate(sets[q], axis=1)) for q in range(4)]
    return [[b[:, j * HALF : (j + 1) * HALF] for b in bins] for j in range(2)]


def first_kernel(starts, own, one, probe, lefts, out, t):
    fill(t, own, one)

    def pair(i, carry):
        for j, bins in enumerate(row_bins(0, (2 * i, 2 * i + 1), starts, t, probe, lefts)):
            for q in range(4):
                out[2 * i + j, q] = bins[q]
        return carry

    lax.fori_loop(0, starts.shape[0] // 2, pair, 0, unroll=2)


def first_half(starts, own, one, beam_probe, lefts):
    return pl.pallas_call(
        first_kernel,
        out_shape=kept((starts.shape[0], 4, 2 * QUARTER, HALF)),
        in_specs=[smem()] + [vmem()] * 4,
        out_specs=vmem(),
        scratch_shapes=[pltpu.VMEM((2, FULL, HALF), f32)],
        compiler_params=params(),
    )(starts, *held(own, one, beam_probe, lefts))


def positions_kernel(starts, mine, two, three, probe, back, amps, lefts, rights, g_out, right_out, left_out, t):
    fill(t, two, three)
    g_out[...] = jnp.zeros(g_out.shape, f32)
    sides = (slice(0, HALF), slice(HALF, BX))
    count = starts.shape[0]
    bins, far_field, change = {}, {}, {}

    def lanes_forward(p):
        even, odd = [], []
        for a, b in zip([mine[p, q] for q in range(4)], bins.pop(p)):
            total, rest = a + b, a - b
            even.append(jnp.concatenate([total[:QUARTER], total[QUARTER:]], axis=1))
            odd.append(jnp.concatenate([rest[:QUARTER], rest[QUARTER:]], axis=1))
        far_field[p] = [along_lanes(stack_rows(*rows), rights[lp]) for lp, rows in ((0, even), (1, odd))]

    def project(p):
        backs = []
        for lp, f in enumerate(far_field.pop(p)):
            fr, fi = f[:, :HALF], f[:, HALF:]
            modulus2 = jnp.maximum(fr * fr + fi * fi, amp_floor * amp_floor)
            factor = amps[p, :, sides[lp]] * lax.rsqrt(modulus2) - 1.0
            backs.append(along_lanes(jnp.concatenate([fr * factor, fi * factor], axis=1), rights[2 + lp]))
        change[p] = backs[0] + backs[1], backs[0] - backs[1]

    def rows_back(p):
        s = starts[p]
        low, high = change.pop(p)
        sets = []
        for q in range(4):
            at = slice(q * QUARTER, (q + 1) * QUARTER)
            stacked = [jnp.concatenate([low[at, side], high[at, side]], axis=1) for side in sides]
            g = along_rows(lefts[4 + q], stack_rows(*stacked))
            sets.append((g[:QUARTER], g[QUARTER:]))
        s0, s1 = both(sets[0], sets[2])
        t0, t1 = both(sets[1], sets[3])
        diff_re = stack_rows(s0[0] + t0[0], s1[0] - t1[1], s0[0] - t0[0], s1[0] + t1[1])
        diff_im = stack_rows(s0[1] + t0[1], s1[1] + t1[0], s0[1] - t0[1], s1[1] - t1[0])
        for turn in range(2):
            dr, di = diff_re[:, sides[turn]], diff_im[:, sides[turn]]
            br, bi = back[0, :, lanes_of(turn)], back[1, :, lanes_of(turn)]
            g_out[0, turn, pl.ds(s, BX), :] += br * dr + bi * di
            g_out[1, turn, pl.ds(s, BX), :] += br * di - bi * dr

    for step in range(count + 3):
        if step < count and step % 2 == 0:
            pair = (step, step + 1)
            bins.update(zip(pair, row_bins(1, pair, starts, t, probe, lefts)))
        if 0 <= step - 1 < count:
            lanes_forward(step - 1)
        if 0 <= step - 2 < count:
            project(step - 2)
        if 0 <= step - 3:
            rows_back(step - 3)
    right_out[...] = g_out[:, :, BX - SH :, :]
    left_out[...] = g_out[:, :, :SH, :]


def positions(starts, mine, two, three, beam_probe, back, amps, lefts, rights):
    return pl.pallas_call(
        positions_kernel,
        out_shape=(kept((2, 2, FULL, HALF)), kept((2, 2, PART, HALF)), kept((2, 2, SH, HALF))),
        in_specs=[smem()] + [vmem()] * 8,
        out_specs=(vmem(), vmem(), vmem()),
        scratch_shapes=[pltpu.VMEM((2, FULL, HALF), f32)],
        compiler_params=params(),
    )(starts, *held(mine, two, three, beam_probe, back, amps, lefts, rights))


EARLY = 3
CHUNKS = BX // SH


def first_early(shear):
    return 3 + (shear > -SH).astype(jnp.int32) + (shear > 0).astype(jnp.int32)


def rows_at(chunk, count, before=0):
    return pl.ds(pl.multiple_of(chunk * SH, SH) + before, count * SH)


def update_layer(z, chunk, count, shear, far, own, changes, before, buf, at):
    for c in range(2):
        for turn, source in enumerate((own, far)):
            cells = source[c, z, rows_at(chunk, count, 2 * SH), :]
            moved = changes[c, turn, pl.ds(chunk * SH + before - shear, count * SH), :]
            buf[c, z, at * SH : (at + count) * SH, lanes_of(turn)] = cells + moved


def send_rows(z, chunk, count, buf, at, out, sem):
    source = buf.at[:, z, pl.ds(at * SH, count * SH), :]
    pltpu.make_async_copy(source, out.at[:, z, rows_at(chunk, count), :], sem).start()


def early_kernel(shears, far, own, g, out, buf, sem):
    def layer(z, carry):
        chunk = first_early(shears[z])
        update_layer(z, chunk, EARLY, shears[z], far, own, g, 0, buf, 0)
        send_rows(z, chunk, EARLY, buf, 0, out, sem)
        return carry

    lax.fori_loop(0, buf.shape[1], layer, 0, unroll=2)
    pltpu.make_async_copy(buf, out.at[:, :, : EARLY * SH, :], sem).wait()


def update_kernel(shears, far, own, g, left, right, begun, out, ext, buf, sem):
    ext[:, :, SH:, :] = g[:, :, : BX + SH, :]
    ext[:, :, :SH, :] = jnp.zeros((2, 2, SH, HALF), f32)
    ext[:, :, :PART, :] += left[...]
    ext[:, :, BX + SH :, :] += right[...]

    def layer(z, carry):
        begin = first_early(shears[z])
        pieces = (
            (0, 3),
            (jnp.where(begin == 3, 6, 3), 1),
            (jnp.where(begin == 5, 4, 7), 1),
        )
        at = 0
        for chunk, count in pieces:
            update_layer(z, chunk, count, shears[z], far, own, ext, SH, buf, at)
            send_rows(z, chunk, count, buf, at, out, sem)
            at += count
        return carry

    lax.fori_loop(0, buf.shape[1], layer, 0, unroll=2)
    pltpu.make_async_copy(buf, out.at[:, :, : (CHUNKS - EARLY) * SH, :], sem).wait()


def update_early(far, own, shears, g):
    layers = far.shape[1]
    return pl.pallas_call(
        early_kernel,
        out_shape=pltpu.HBM((2, layers, BX, BX), f32),
        in_specs=[smem()] + [vmem()] * 3,
        out_specs=pl.BlockSpec(memory_space=pltpu.HBM),
        scratch_shapes=[pltpu.VMEM((2, layers, EARLY * SH, BX), f32), pltpu.SemaphoreType.DMA],
        compiler_params=params(),
    )(shears, *held(far, own, g))


def update(far, own, shears, g, left, right, begun):
    layers = far.shape[1]
    return pl.pallas_call(
        update_kernel,
        out_shape=jax.ShapeDtypeStruct((2, layers, BX, BX), f32),
        in_specs=[smem()] + [vmem()] * 5 + [pl.BlockSpec(memory_space=pltpu.HBM)],
        out_specs=pl.BlockSpec(memory_space=pltpu.HBM),
        input_output_aliases={6: 0},
        scratch_shapes=[
            pltpu.VMEM((2, 2, BX + 2 * SH, HALF), f32),
            pltpu.VMEM((2, layers, (CHUNKS - EARLY) * SH, BX), f32),
            pltpu.SemaphoreType.DMA,
        ],
        compiler_params=params(),
    )(shears, *held(far, own, g, left, right), begun)


def depth_swap(value, by):
    return lax.ppermute(value, "dep", [(i, i ^ by) for i in range(DEP)])


def shifted(value, by):
    count = lax.axis_size("lat")
    return lax.ppermute(value, "lat", [(i, i + by) for i in range(count) if 0 <= i + by < count])


def body(crystal, beam_probe, amplitudes, starts, shears):
    lefts, rights, pick = packed_tables()
    send2, send3, far = partial_sums(crystal, shears, True)
    got3 = depth_swap(send3, 3)
    got2 = depth_swap(send2, 2)
    send1, mine, near_half = partial_sums(crystal, shears, False, send2)
    got1 = depth_swap(send1, 1)
    amps, back = prepare(amplitudes, beam_probe, pick)
    part = sum_blocks(mine, got1, got2, got3, back)
    whole, to_left, to_right = edges(part, depth_swap(part, 4))
    block = finish(whole, shifted(to_right, 1), shifted(to_left, -1))
    three = depth_swap(block, 3)
    two = depth_swap(block, 2)
    one = depth_swap(block, 1)
    bins = first_half(starts, block, one, beam_probe, lefts)
    g, to_right, to_left = positions(starts, bins, two, three, beam_probe, back, amps, lefts, rights)
    begun = update_early(far, near_half, shears, g)
    return update(far, near_half, shears, g, shifted(to_right, 1), shifted(to_left, -1), begun)


def solution(mesh):
    placed = (P(None, "dep", "lat", None), P(), P("lat", None, None), P("lat"), P("dep"))
    return jax.shard_map(
        body, mesh=mesh, in_specs=placed, out_specs=P(None, "dep", "lat", None), check_vma=False
    )
```
